512 devices in a mesh: seq: 16 (over y, z_hi), mp: 8 (over z_lo, core), leaf: 4 (over x).
Axes of the slice: x: 4, y: 8, z: 8 (z_hi: 2, z_lo: 4; z = z_hi * 4 + z_lo), core: 2. Of those that a mesh axis runs over, the one named last changes fastest.
Arguments:
- queries: bfloat16 [16384, 8192], P(('leaf', 'seq'), 'mp'), parts along dimension 0
- keys: bfloat16 [16384, 1024], P(('leaf', 'seq'), 'mp'), parts along dimension 0
- values: bfloat16 [16384, 1024], P(('leaf', 'seq'), 'mp'), parts along dimension 0, may hold values from -5 to 5
- tree_mask: int32 [64, 16], P('leaf'), parts along dimension 0, may hold values from 0 to 1, as said below
- step_lengths: int32 [64], P('leaf'), parts along dimension 0, may hold values from 2 to 256, as said below
- probe: bfloat16 [8192], P('mp'), may hold values from -0.5 to 0.5
Outputs:
- attended: bfloat16 [16384, 8192], P(('leaf', 'seq'), 'mp'), parts along dimension 0
- step_score: float32 [64], P(('leaf', 'seq')), parts along dimension 0
The draws below stay inside these ranges and needn't reach their ends.
There are 4 independent parts, one for each index of `leaf`. The reference program is written for one: setup_inputs(seed, part) draws one part's arguments, and reference() takes and returns one part's arrays. A program takes and returns all parts, laid end to end along the dimension named above; an argument that names none is the same for every part. Nothing has to cross between parts.
Inputs may be any that keep to these rules, and one draw needn't show every extreme that they name: Block 0 is the root: tree_mask[i, 0] = 1 for every i; tree_mask[i, i] = 1; every other block's ancestors have lower indices than it, and the ancestors of an ancestor are ancestors too. `step_lengths`: some block uses all 256 slots.
All inputs are finite; a program needn't handle non-finite values.
Results may differ from the reference program's by a relative error of at most 0.015.
Values may be sent and summed in bfloat16 or wider, within the bound.
No kernel may reach another device: no remote copies, remote signals or barrier semaphores. Data moves between devices by JAX's collectives and lax.ppermute only.
A program may use at most 64 MiB of HBM per device.

```python
import jax
import jax.numpy as jnp
from jax import lax

H = 64
KVH = 8
DH = 128
BLOCK = 256
NB = 16
TOKENS = 4096


def draw_queries(key, part):
    key = jax.random.fold_in(key, 1)
    return jax.random.truncated_normal(key, -4.0, 4.0, (TOKENS, H * DH), jnp.float32).astype(jnp.bfloat16)


def draw_keys(key, part):
    key = jax.random.fold_in(key, 2)
    return jax.random.truncated_normal(key, -4.0, 4.0, (TOKENS, KVH * DH), jnp.float32).astype(jnp.bfloat16)


def draw_tree_mask(key, part):
    key = jax.random.fold_in(key, 7)
    first, second, third = jax.random.split(key, 3)
    index = jnp.arange(NB)
    upper = jnp.maximum(index, 1)
    left = jax.random.randint(first, (NB,), 0, upper)
    right = jax.random.randint(second, (NB,), 0, upper)
    deeper = jax.random.randint(third, (NB,), 0, 2)
    parent = jnp.where(deeper == 1, jnp.maximum(left, right), jnp.minimum(left, right))
    parent = jnp.where(index == 0, 0, parent)
    ident = jnp.eye(NB, dtype=jnp.int32)

    def extend(step, mask):
        inherited = jnp.where((index == 0)[:, None], ident, mask[parent])
        return jnp.maximum(ident, inherited)
    return lax.fori_loop(0, NB, extend, ident)


def draw_step_lengths(key, part):
    key = jax.random.fold_in(key, 5)
    first, second = jax.random.split(key)
    lengths = jax.random.randint(first, (NB,), 2, BLOCK + 1)
    chosen = jax.random.randint(second, (), 0, NB)
    return jnp.where(jnp.arange(NB) == chosen, BLOCK, lengths).astype(jnp.int32)


def level_of(rng, shape, cuts, low, high):
    loudness = 1.0
    for dim, blocks in cuts:
        steps = jax.random.uniform(jax.random.fold_in(jax.random.fold_in(rng, 6), dim), (blocks,), jnp.float32, low / len(cuts), high / len(cuts))
        loudness = loudness * jnp.repeat(jnp.exp(steps), shape[dim] // blocks).reshape((-1,) + (1,) * (len(shape) - 1 - dim))
    return loudness


def gaussian(key, shape, deviation, bound, shards=(), held_as=jnp.bfloat16):
    gain = level_of(key, shape, shards, -0.22, 0.18) if shards else 1.0
    values = jax.random.normal(key, shape, jnp.float32) * deviation * gain
    return jnp.minimum(jnp.maximum(values, -bound), bound).astype(held_as)


def setup_inputs(seed: int = 0, part: int = 0) -> dict:
    key_list = jax.random.split(jax.random.key(seed), 7)
    part_keys = jax.random.split(jax.random.fold_in(key_list[6], part), 7)
    queries = draw_queries(jax.random.fold_in(jax.random.fold_in(key_list[6], part), 71), part)
    keys = draw_keys(jax.random.fold_in(jax.random.fold_in(key_list[6], part), 71), part)
    values = gaussian(part_keys[2], (TOKENS, KVH * DH), 1.0, 5.0, ((0, 16), (1, 8)))
    tree_mask = draw_tree_mask(jax.random.fold_in(jax.random.fold_in(key_list[6], part), 71), part)
    step_lengths = draw_step_lengths(jax.random.fold_in(jax.random.fold_in(key_list[6], part), 71), part)
    probe = gaussian(key_list[5], (H * DH,), 0.1, 0.5, ((0, 8),))
    return dict(queries=queries, keys=keys, values=values, tree_mask=tree_mask, step_lengths=step_lengths, probe=probe)


def reference(queries, keys, values, tree_mask, step_lengths, probe):
    group = H // KVH
    scale = 1.0 / (DH ** 0.5)
    token_ids = jnp.arange(TOKENS).astype(jnp.int32)
    tok_block = token_ids // BLOCK
    tok_pos = token_ids % BLOCK
    key_valid = tok_pos < step_lengths[tok_block]
    query_blocks = queries.reshape(NB, BLOCK, KVH, group, DH)
    key_heads = keys.reshape(TOKENS, KVH, DH).astype(jnp.float32)
    value_heads = values.reshape(TOKENS, KVH, DH).astype(jnp.float32)
    row_pos = jnp.arange(BLOCK).astype(jnp.int32)

    def one_block(block):
        query_rows = lax.dynamic_index_in_dim(query_blocks, block, 0, keepdims=False).astype(jnp.float32)
        ancestor = lax.dynamic_index_in_dim(tree_mask, block, 0, keepdims=False)[tok_block] > 0
        causal = (tok_block != block)[None, :] | (tok_pos[None, :] <= row_pos[:, None])
        allowed = (ancestor & key_valid)[None, :] & causal
        allowed = allowed[:, None, None, :]
        scores = jnp.einsum("rkgd,tkd->rkgt", query_rows, key_heads) * scale
        scores = jnp.where(allowed, scores, -1e30)
        top = jnp.max(scores, axis=-1)
        weights = jnp.where(allowed, jnp.exp(scores - top[..., None]), 0.0)
        total = jnp.sum(weights, axis=-1)
        rounded = weights.astype(jnp.bfloat16).astype(jnp.float32)
        mixed = jnp.einsum("rkgt,tkd->rkgd", rounded, value_heads) / total[..., None]
        length = lax.dynamic_index_in_dim(step_lengths, block, 0, keepdims=False)
        mixed = jnp.where((row_pos < length)[:, None, None, None], mixed, 0.0)
        return mixed.reshape(BLOCK, H * DH).astype(jnp.bfloat16)

    attended = lax.map(one_block, jnp.arange(NB).astype(jnp.int32)).reshape(TOKENS, H * DH)
    last_rows = (jnp.arange(NB).astype(jnp.int32) * BLOCK + step_lengths - 1).astype(jnp.int32)
    picked = attended[last_rows].astype(jnp.float32)
    step_score = jnp.sum(picked * probe.astype(jnp.float32)[None, :], axis=-1)
    return attended, step_score
```

```python
import functools
import math

import jax
import jax.numpy as jnp
from jax import lax
from jax.experimental import pallas as pl
from jax.experimental.pallas import tpu as pltpu
from jax.sharding import PartitionSpec as P

DH = 128
BLOCK = 256
CHUNK = 16
PAIR = 2 * CHUNK
NEG = -1e30

VMEM = pltpu.VMEM
SMEM = pltpu.SMEM


def chunks_of(length):
    return (length + CHUNK - 1) // CHUNK


def plan_kernel(planes, sizes, mask_ref, len_ref, k_ref, v_ref, send_ref, meta_ref):
    nblocks = mask_ref.shape[0]
    holders = nblocks // planes
    me = lax.axis_index("seq")
    counts = [chunks_of(len_ref[b]) for b in range(nblocks)]
    most = jnp.int32(0)
    my_start = jnp.int32(0)
    for b in range(nblocks):
        for plane in range(planes):
            total = jnp.int32(0)
            for a in range(plane, b, planes):
                total += jnp.where(mask_ref[b, a] > 0, counts[a], 0)
            most = jnp.maximum(most, total)
            if plane == b % planes:
                meta_ref[b] = total
                my_start = jnp.where(me == b, total, my_start)
    slots = (most + holders - 1) // holders
    choice = jnp.int32(0)
    for size in sizes[:-1]:
        choice += jnp.where(slots > size, 1, 0)
    meta_ref[nblocks] = choice
    per = BLOCK // CHUNK // holders
    for chunk in range(BLOCK // CHUNK):
        holder = lax.rem(my_start + chunk, holders)
        row = (chunk // holders) * PAIR
        rows = slice(chunk * CHUNK, (chunk + 1) * CHUNK)
        send_ref[holder, row : row + CHUNK, :] = k_ref[rows, :]
        send_ref[holder, row + CHUNK : row + PAIR, :] = v_ref[rows, :]


def pack_kernel(planes, slots, mask_ref, len_ref, meta_ref, held_ref, send_ref):
    nblocks = mask_ref.shape[0]
    holders = nblocks // planes
    me = lax.axis_index("seq")
    mine, plane = me // planes, lax.rem(me, planes)
    send_ref[...] = jnp.zeros_like(send_ref)
    for y in range(holders):
        block = y * planes + plane
        start = meta_ref[block]
        count = chunks_of(len_ref[block])
        first = lax.rem(mine - start + BLOCK, holders)
        for k in range(BLOCK // CHUNK // holders):
            chunk = first + k * holders
            row = pl.multiple_of((start + chunk) // holders * PAIR, PAIR)

            @pl.when(chunk < count)
            def _():
                piece = held_ref[y, k * PAIR : (k + 1) * PAIR, :]
                for j in range(y * planes + 1, nblocks):

                    @pl.when((mask_ref[j, block] > 0) & (block < j))
                    def _():
                        send_ref[j, pl.ds(row, PAIR), :] = piece


def attend_kernel(
    planes, slots, mask_ref, len_ref, meta_ref, q_ref, k_ref, v_ref, got_ref, probe_ref, out_ref, score_ref,
    keys, vals, bias,
):
    nblocks = mask_ref.shape[0]
    me = lax.axis_index("seq")
    length = len_ref[me]
    scale = 1.0 / math.sqrt(DH)
    width = nblocks * CHUNK
    lane = lax.broadcasted_iota(jnp.int32, (slots, width), 1)
    slot = lax.broadcasted_iota(jnp.int32, (slots, width), 0)
    source = lane // CHUNK
    where_row = (slot * (nblocks // planes) + source // planes) * CHUNK + lane % CHUNK
    of_plane = source % planes
    allowed = jnp.zeros((slots, width), jnp.bool_)
    for b in range(nblocks - 1):
        used = jnp.where((mask_ref[me, b] > 0) & (b != me), len_ref[b], 0)
        row = where_row - meta_ref[b] * CHUNK
        allowed |= (of_plane == b % planes) & (row >= 0) & (row < used)
    bias[...] = jnp.where(allowed, 0.0, NEG)
    for s in range(slots):
        for i in range(nblocks):
            at = s * width + i * CHUNK
            keys[at : at + CHUNK, :] = got_ref[i, s * PAIR : s * PAIR + CHUNK, :]
            vals[at : at + CHUNK, :] = got_ref[i, s * PAIR + CHUNK : (s + 1) * PAIR, :]
    row_id = lax.broadcasted_iota(jnp.int32, (BLOCK, 1), 0)
    causal = lax.broadcasted_iota(jnp.int32, (BLOCK, BLOCK), 1) <= row_id
    nt = (((1,), (1,)), ((), ()))
    nheads = q_ref.shape[1] // DH

    def one_head(h, carry):
        columns = pl.ds(pl.multiple_of(h * DH, DH), DH)
        q = q_ref[:, columns]
        own = lax.dot_general(q, k_ref[...], nt, preferred_element_type=jnp.float32)
        parts = [jnp.where(causal, own, NEG)]
        for s in range(slots):
            part = lax.dot_general(
                q, keys[s * width : (s + 1) * width, :], nt, preferred_element_type=jnp.float32
            )
            parts.append(part + bias[s : s + 1, :])
        top = functools.reduce(jnp.maximum, [jnp.max(p, axis=1, keepdims=True) for p in parts])
        total = jnp.zeros((BLOCK, 1), jnp.float32)
        acc = jnp.zeros((BLOCK, DH), jnp.float32)
        for n, part in enumerate(parts):
            w = jnp.exp((part - top) * scale)
            total += jnp.sum(w, axis=1, keepdims=True)
            v = v_ref[...] if n == 0 else vals[(n - 1) * width : n * width, :]
            acc += jnp.dot(w.astype(jnp.bfloat16), v, preferred_element_type=jnp.float32)
        out_ref[:, columns] = jnp.where(row_id < length, acc / total, 0.0).astype(out_ref.dtype)
        return carry

    lax.fori_loop(0, nheads, one_head, 0)
    last = length - 1
    base = pl.multiple_of(last // CHUNK * CHUNK, CHUNK)
    rows = out_ref[pl.ds(base, CHUNK), :].astype(jnp.float32)
    picked = lax.broadcasted_iota(jnp.int32, (CHUNK, 1), 0) == last - base
    part = jnp.where(picked, rows, 0.0) * probe_ref[...].astype(jnp.float32)
    score_ref[...] = jnp.full(score_ref.shape, jnp.sum(part), jnp.float32)


def on_device(planes, queries, keys, values, tree_mask, step_lengths, probe):
    nblocks = tree_mask.shape[0]
    holders = nblocks // planes
    sizes = [s for s in (2, 3, 4, 5, 6, 7, 8, 10, 12, 16)]
    smem, vmem = pl.BlockSpec(memory_space=SMEM), pl.BlockSpec(memory_space=VMEM)
    per = BLOCK // CHUNK // holders
    send, meta = pl.pallas_call(
        functools.partial(plan_kernel, planes, sizes),
        out_shape=(
            jax.ShapeDtypeStruct((holders, per * PAIR, DH), jnp.bfloat16),
            jax.ShapeDtypeStruct((nblocks + 1,), jnp.int32),
        ),
        in_specs=[smem, smem, vmem, vmem],
        out_specs=(vmem, smem),
    )(tree_mask, step_lengths, keys, values)
    groups = [[y * planes + p for y in range(holders)] for p in range(planes)]
    held = lax.all_to_all(send, "seq", 0, 0, axis_index_groups=groups)

    def rest(slots, held, meta):
        packed = pl.pallas_call(
            functools.partial(pack_kernel, planes, slots),
            out_shape=jax.ShapeDtypeStruct((nblocks, slots * PAIR, DH), jnp.bfloat16),
            in_specs=[smem, smem, smem, vmem],
            out_specs=vmem,
        )(tree_mask, step_lengths, meta, held)
        got = lax.all_to_all(packed, "seq", 0, 0)
        rows = slots * nblocks * CHUNK
        return pl.pallas_call(
            functools.partial(attend_kernel, planes, slots),
            out_shape=(
                jax.ShapeDtypeStruct(queries.shape, jnp.bfloat16),
                jax.ShapeDtypeStruct((8, 1, 128), jnp.float32),
            ),
            in_specs=[smem, smem, smem, vmem, vmem, vmem, vmem, vmem],
            out_specs=(vmem, vmem),
            scratch_shapes=[
                VMEM((rows, DH), jnp.bfloat16),
                VMEM((rows, DH), jnp.bfloat16),
                VMEM((slots, nblocks * CHUNK), jnp.float32),
            ],
            compiler_params=pltpu.CompilerParams(vmem_limit_bytes=48 * 1024 * 1024),
        )(tree_mask, step_lengths, meta, queries, keys, values, got, probe.reshape(1, -1))

    branches = [functools.partial(rest, s) for s in sizes]
    attended, score = lax.switch(meta[nblocks], branches, held, meta)
    parts = lax.all_to_all(score, "mp", 0, 0)
    return attended, jnp.sum(parts[:, 0, :1], axis=0)


def solution(mesh):
    in_specs = (
        P(("leaf", "seq"), "mp"),
        P(("leaf", "seq"), "mp"),
        P(("leaf", "seq"), "mp"),
        P("leaf", None),
        P("leaf"),
        P("mp"),
    )
    out_specs = (P(("leaf", "seq"), "mp"), P(("leaf", "seq")))
    return jax.shard_map(
        functools.partial(on_device, 2), mesh=mesh, in_specs=in_specs, out_specs=out_specs, check_vma=False
    )
```

```python
import functools
import math

import jax
import jax.numpy as jnp
from jax import lax
from jax.experimental import pallas as pl
from jax.experimental.pallas import tpu as pltpu
from jax.sharding import PartitionSpec as P

DH = 128
BLOCK = 256
CHUNK = 16
PAIR = 2 * CHUNK
PER_KEYS = BLOCK // CHUNK
NEG = -1e30
NT = (((1,), (1,)), ((), ()))
SIZES = (3, 4, 5, 6, 7, 8, 11, 16)

VMEM = pltpu.VMEM
SMEM = pltpu.SMEM


def chunks_of(length):
    return (length + CHUNK - 1) // CHUNK


def spread_kernel(planes, mask_ref, len_ref, k_ref, v_ref, send_ref):
    nblocks = mask_ref.shape[0]
    holders = nblocks // planes
    me = lax.axis_index("seq")
    start = jnp.int32(0)
    for a in range(nblocks - 1):
        counted = (a < me) & (lax.rem(me, planes) == a % planes)
        start += jnp.where(counted, mask_ref[me, a] * chunks_of(len_ref[a]), 0)
    for chunk in range(PER_KEYS):
        holder = lax.rem(start + chunk, holders)
        row = (chunk // holders) * PAIR
        rows = slice(chunk * CHUNK, (chunk + 1) * CHUNK)
        send_ref[holder, row : row + CHUNK, :] = k_ref[rows, :]
        send_ref[holder, row + CHUNK : row + PAIR, :] = v_ref[rows, :]


def table_kernel(planes, mask_ref, len_ref, meta_ref, choice_ref):
    nblocks = mask_ref.shape[0]
    holders = nblocks // planes
    me = lax.axis_index("seq")
    counts = [chunks_of(len_ref[b]) for b in range(nblocks)]
    most = jnp.int32(0)
    mine = [jnp.int32(0) for _ in range(planes)]
    for b in range(nblocks):
        for plane in range(planes):
            total = jnp.int32(0)
            for a in range(plane, b, planes):
                total += mask_ref[b, a] * counts[a]
            most = jnp.maximum(most, total)
            mine[plane] = jnp.where(me == b, total, mine[plane])
            if plane == b % planes:
                meta_ref[b] = total
    for plane in range(planes):
        meta_ref[nblocks + plane] = mine[plane]
    slots = (most + holders - 1) // holders
    choice = jnp.int32(0)
    for size in SIZES[:-1]:
        choice += jnp.where(slots > size, 1, 0)
    choice_ref[0] = choice


def pack_kernel(planes, slots, mask_ref, len_ref, meta_ref, held_ref, send_ref, work):
    nblocks = mask_ref.shape[0]
    holders = nblocks // planes
    me = lax.axis_index("seq")
    mine, plane = me // planes, lax.rem(me, planes)
    work[...] = jnp.zeros_like(work)

    for y in range(holders):
        block = y * planes + plane
        start = meta_ref[block]
        count = chunks_of(len_ref[block])
        first = lax.rem(mine - start + BLOCK, holders)
        for k in range(PER_KEYS // holders):
            chunk = first + k * holders
            slot = jnp.minimum((start + chunk) // holders, slots - 1)
            row = pl.multiple_of(slot * PAIR, PAIR)
            used = jnp.where(chunk < count, 1, 0)
            piece = held_ref[y, k * PAIR : (k + 1) * PAIR, :]
            for j in range(y * planes + 1, nblocks):
                needed = mask_ref[j, block] * used
                if j < (y + 1) * planes:
                    needed = jnp.where(block < j, needed, 0)
                work[jnp.where(needed > 0, j, nblocks), pl.ds(row, PAIR), :] = piece
    send_ref[...] = work[:nblocks]


def own_kernel(
    planes, slots, mask_ref, len_ref, meta_ref, q_ref, k_ref, v_ref, probe_ref,
    top_ref, total_ref, acc_ref, across_ref, down_ref, lastq_ref, probes_ref, own_s_ref, own_p_ref, vt,
):
    nblocks = mask_ref.shape[0]
    me = lax.axis_index("seq")
    length = len_ref[me]
    nheads = q_ref.shape[1] // DH
    scale = 1.0 / math.sqrt(DH)
    row_at = lax.broadcasted_iota(jnp.int32, (slots, BLOCK), 0) * BLOCK
    row_at = row_at + lax.broadcasted_iota(jnp.int32, (slots, BLOCK), 1)
    row_id = lax.broadcasted_iota(jnp.int32, (CHUNK, DH), 0)
    allowed = jnp.zeros((slots, BLOCK), jnp.int32)
    down_ref[...] = jnp.full(down_ref.shape, NEG, jnp.float32)
    for b in range(nblocks - 1):
        before = meta_ref[b]
        for plane in range(b % planes):
            before += meta_ref[nblocks + plane]
        used = jnp.where((mask_ref[me, b] > 0) & (b < me), len_ref[b], 0)
        row = row_at - before * CHUNK
        allowed = jnp.where((row >= 0) & (row < used), 1, allowed)

        def one_chunk(c, carry):
            at = pl.multiple_of((before + c) * CHUNK, CHUNK)
            down_ref[pl.ds(at, CHUNK), :] = jnp.where(row_id < used - c * CHUNK, 0.0, NEG)
            return carry

        lax.fori_loop(0, chunks_of(used), one_chunk, 0)
    across_ref[...] = jnp.where(allowed > 0, 0.0, NEG)
    causal = lax.broadcasted_iota(jnp.int32, (BLOCK, BLOCK), 0) <= lax.broadcasted_iota(
        jnp.int32, (BLOCK, BLOCK), 1
    )
    vt[...] = jnp.transpose(v_ref[...].astype(jnp.float32)).astype(jnp.bfloat16)
    last = length - 1
    base = pl.multiple_of(last // CHUNK * CHUNK, CHUNK)
    picked = lax.broadcasted_iota(jnp.int32, (CHUNK, 1), 0) == last - base

    def one_head(h, carry):
        columns = pl.ds(pl.multiple_of(h * DH, DH), DH)
        scores = lax.dot_general(k_ref[...], q_ref[:, columns], NT, preferred_element_type=jnp.float32)
        scores = jnp.where(causal, scores, NEG)
        top = jnp.max(scores, axis=0, keepdims=True)
        w = jnp.exp((scores - top) * scale)
        top_ref[h] = top
        total_ref[h] = jnp.sum(w, axis=0, keepdims=True)
        acc_ref[h] = jnp.dot(vt[...], w.astype(jnp.bfloat16), preferred_element_type=jnp.float32)
        return carry

    lax.fori_loop(0, nheads, one_head, 0)
    for h in range(nheads):
        columns = slice(h * DH, (h + 1) * DH)
        near = q_ref[pl.ds(base, CHUNK), columns].astype(jnp.float32)
        lastq_ref[h : h + 1, :] = jnp.sum(jnp.where(picked, near, 0.0), axis=0, keepdims=True)
        probes_ref[h : h + 1, :] = probe_ref[:, columns].astype(jnp.float32)
    lastq = lastq_ref[...].astype(jnp.bfloat16)
    probes = probes_ref[...].astype(jnp.bfloat16)
    own_s = lax.dot_general(lastq, k_ref[...], NT, preferred_element_type=jnp.float32)
    inside = lax.broadcasted_iota(jnp.int32, (1, BLOCK), 1) < length
    own_s_ref[...] = jnp.where(inside, own_s, NEG)
    own_p_ref[...] = lax.dot_general(probes, v_ref[...], NT, preferred_element_type=jnp.float32)


def score_kernel(
    planes, slots, meta_ref, got_ref, across_ref, lastq_ref, probes_ref, own_s_ref, own_p_ref, score_ref, keys_ref, vals_ref,
):
    nblocks = got_ref.shape[0]
    holders = nblocks // planes
    scale = 1.0 / math.sqrt(DH)
    zeros = jnp.zeros((BLOCK, DH), jnp.bfloat16)
    before = jnp.int32(0)
    for plane in range(planes):
        tail = pl.multiple_of((before + slots * holders) * CHUNK, CHUNK)
        if plane == 0:
            keys_ref[slots * holders * CHUNK :, :] = jnp.zeros_like(keys_ref[slots * holders * CHUNK :, :])
            vals_ref[slots * holders * CHUNK :, :] = jnp.zeros_like(vals_ref[slots * holders * CHUNK :, :])
        else:
            keys_ref[pl.ds(tail, BLOCK), :] = zeros
            vals_ref[pl.ds(tail, BLOCK), :] = zeros
        for s in range(slots):
            for p in range(holders):
                at = pl.multiple_of((before + s * holders + p) * CHUNK, CHUNK)
                i = p * planes + plane
                keys_ref[pl.ds(at, CHUNK), :] = got_ref[i, s * PAIR : s * PAIR + CHUNK, :]
                vals_ref[pl.ds(at, CHUNK), :] = got_ref[i, s * PAIR + CHUNK : (s + 1) * PAIR, :]
        before += meta_ref[nblocks + plane]
    lastq = lastq_ref[...].astype(jnp.bfloat16)
    probes = probes_ref[...].astype(jnp.bfloat16)
    scores, products = [own_s_ref[...]], [own_p_ref[...]]
    for s in range(slots):
        rows = slice(s * BLOCK, (s + 1) * BLOCK)
        part = lax.dot_general(lastq, keys_ref[rows, :], NT, preferred_element_type=jnp.float32)
        scores.append(part + across_ref[s : s + 1, :])
        products.append(
            lax.dot_general(probes, vals_ref[rows, :], NT, preferred_element_type=jnp.float32)
        )
    top = jnp.max(functools.reduce(jnp.maximum, scores), axis=1, keepdims=True)
    weights = [jnp.exp((part - top) * scale) for part in scores]
    total = jnp.sum(sum(weights), axis=1, keepdims=True)
    mixed = jnp.sum(sum(w * p for w, p in zip(weights, products)), axis=1, keepdims=True)
    score_ref[...] = jnp.full(score_ref.shape, jnp.sum(mixed / total), jnp.float32)


def attend_kernel(
    planes, slots, len_ref, meta_ref, q_ref, keys_ref, vals_ref, down_ref, top_ref, total_ref, acc_ref, out_ref,
    kept, tops, totals, accs,
):
    length = len_ref[lax.axis_index("seq")]
    nblocks = len_ref.shape[0]
    nheads = q_ref.shape[1] // DH
    scale = 1.0 / math.sqrt(DH)
    count = jnp.int32(0)
    for plane in range(planes):
        count += meta_ref[nblocks + plane]
    steps = (count + PER_KEYS - 1) // PER_KEYS
    for h in range(nheads):
        tops[h] = jnp.broadcast_to(top_ref[h], (8, BLOCK))

    def one_score(n, carry):
        at = pl.ds(pl.multiple_of(n * BLOCK, BLOCK), BLOCK)
        bias = down_ref[at, :]
        bias = jnp.concatenate([bias, bias], axis=1)
        for h in range(nheads):
            q = q_ref[:, h * DH : (h + 1) * DH]
            part = lax.dot_general(keys_ref[at, :], q, NT, preferred_element_type=jnp.float32) + bias
            kept[n, h] = part
            tops[h] = jnp.maximum(tops[h], jnp.max(part.reshape(BLOCK // 8, 8, BLOCK), axis=0))
        return carry

    lax.fori_loop(0, steps, one_score, 0)
    for h in range(nheads):
        top = jnp.max(tops[h], axis=0, keepdims=True)
        tops[h] = jnp.broadcast_to(top, (8, BLOCK))
        factor = jnp.exp((top_ref[h] - top) * scale)
        row = lax.broadcasted_iota(jnp.int32, (8, BLOCK), 0)
        totals[h] = jnp.where(row == 0, total_ref[h] * factor, 0.0)
        accs[h] = acc_ref[h] * factor

    def one_mix(n, carry):
        at = pl.ds(pl.multiple_of(n * BLOCK, BLOCK), BLOCK)
        vt = jnp.transpose(vals_ref[at, :].astype(jnp.float32)).astype(jnp.bfloat16)
        for h in range(nheads):
            w = jnp.exp((kept[n, h] - tops[h, :1, :]) * scale)
            totals[h] += jnp.sum(w.reshape(BLOCK // 8, 8, BLOCK), axis=0)
            accs[h] += jnp.dot(vt, w.astype(jnp.bfloat16), preferred_element_type=jnp.float32)
        return carry

    lax.fori_loop(0, steps, one_mix, 0)
    row_id = lax.broadcasted_iota(jnp.int32, (BLOCK, 1), 0)
    for h in range(nheads):
        total = jnp.sum(totals[h], axis=0, keepdims=True)
        result = jnp.transpose(accs[h] / total)
        out_ref[:, h * DH : (h + 1) * DH] = jnp.where(row_id < length, result, 0.0).astype(out_ref.dtype)


def on_device(planes, queries, keys, values, tree_mask, step_lengths, probe):
    nblocks = tree_mask.shape[0]
    holders = nblocks // planes
    nheads = queries.shape[1] // DH
    smem, vmem = pl.BlockSpec(memory_space=SMEM), pl.BlockSpec(memory_space=VMEM)
    f32, bf16 = jnp.float32, jnp.bfloat16
    shape = jax.ShapeDtypeStruct
    limit = lambda mib: pltpu.CompilerParams(vmem_limit_bytes=mib * 1024 * 1024)
    send = pl.pallas_call(
        functools.partial(spread_kernel, planes),
        out_shape=shape((holders, PER_KEYS // holders * PAIR, DH), bf16),
        in_specs=[smem, smem, vmem, vmem],
        out_specs=vmem,
        compiler_params=limit(8),
    )(tree_mask, step_lengths, keys, values)
    groups = [[y * planes + p for y in range(holders)] for p in range(planes)]
    held = lax.all_to_all(send, "seq", 0, 0, axis_index_groups=groups)
    meta, choice = pl.pallas_call(
        functools.partial(table_kernel, planes),
        out_shape=(shape((nblocks + planes,), jnp.int32), shape((1,), jnp.int32)),
        in_specs=[smem, smem],
        out_specs=(smem, smem),
        cost_estimate=pl.CostEstimate(flops=10**8, bytes_accessed=10**5, transcendentals=0),
        compiler_params=limit(8),
    )(tree_mask, step_lengths)

    def rest(slots, held, meta):
        packed = pl.pallas_call(
            functools.partial(pack_kernel, planes, slots),
            out_shape=shape((nblocks, slots * PAIR, DH), bf16),
            in_specs=[smem, smem, smem, vmem],
            out_specs=vmem,
            scratch_shapes=[VMEM((nblocks + 1, slots * PAIR, DH), bf16)],
            compiler_params=limit(16),
        )(tree_mask, step_lengths, meta, held)
        got = lax.all_to_all(packed, "seq", 0, 0)
        per_head = shape((nheads, 1, BLOCK), f32)
        small = shape((nheads, DH), f32)
        top, total, acc, across, down, lastq, probes, own_s, own_p = pl.pallas_call(
            functools.partial(own_kernel, planes, slots),
            out_shape=(
                per_head, per_head, shape((nheads, DH, BLOCK), f32), shape((slots, BLOCK), f32),
                shape((slots * BLOCK, DH), f32), small, small,
                shape((nheads, BLOCK), f32), shape((nheads, BLOCK), f32),
            ),
            in_specs=[smem, smem, smem, vmem, vmem, vmem, vmem],
            out_specs=(vmem,) * 9,
            scratch_shapes=[VMEM((DH, BLOCK), bf16)],
            cost_estimate=pl.CostEstimate(flops=10**9, bytes_accessed=5 * 10**6, transcendentals=10**6),
            compiler_params=limit(12),
        )(tree_mask, step_lengths, meta, queries, keys, values, probe.reshape(1, -1))
        together = shape((slots * BLOCK + BLOCK, DH), bf16)
        score, all_keys, all_vals = pl.pallas_call(
            functools.partial(score_kernel, planes, slots),
            out_shape=(shape((lax.axis_size("mp"), 1, DH), f32), together, together),
            in_specs=[smem] + [vmem] * 6,
            out_specs=(vmem, vmem, vmem),
            compiler_params=limit(16),
        )(meta, got, across, lastq, probes, own_s, own_p)
        parts = lax.all_to_all(score, "mp", 0, 0)
        attended = pl.pallas_call(
            functools.partial(attend_kernel, planes, slots),
            out_shape=shape(queries.shape, bf16),
            in_specs=[smem, smem] + [vmem] * 7,
            out_specs=vmem,
            scratch_shapes=[
                VMEM((slots, nheads, BLOCK, BLOCK), f32),
                VMEM((nheads, 8, BLOCK), f32),
                VMEM((nheads, 8, BLOCK), f32),
                VMEM((nheads, DH, BLOCK), f32),
            ],
            cost_estimate=pl.CostEstimate(flops=4 * 10**9, bytes_accessed=5 * 10**6, transcendentals=4 * 10**6),
            compiler_params=limit(10 + 2 * slots),
        )(step_lengths, meta, queries, all_keys, all_vals, down, top, total, acc)
        return attended, parts

    branches = [functools.partial(rest, s) for s in SIZES]
    attended, parts = lax.switch(choice[0], branches, held, meta)
    return attended, jnp.sum(parts[:, 0, :1], axis=0)


def solution(mesh):
    in_specs = (
        P(("leaf", "seq"), "mp"),
        P(("leaf", "seq"), "mp"),
        P(("leaf", "seq"), "mp"),
        P("leaf", None),
        P("leaf"),
        P("mp"),
    )
    out_specs = (P(("leaf", "seq"), "mp"), P(("leaf", "seq")))
    return jax.shard_map(
        functools.partial(on_device, 2), mesh=mesh, in_specs=in_specs, out_specs=out_specs, check_vma=False
    )
```

```python
import functools
import math

import jax
import jax.numpy as jnp
from jax import lax
from jax.experimental import pallas as pl
from jax.experimental.pallas import tpu as pltpu
from jax.sharding import PartitionSpec as P

DH = 128
BLOCK = 256
CHUNK = 16
PAIR = 2 * CHUNK
PER_KEYS = BLOCK // CHUNK
NEG = -1e30
NT = (((1,), (1,)), ((), ()))
SIZES = (3, 4, 5, 6, 7, 8, 11, 16)

VMEM = pltpu.VMEM
SMEM = pltpu.SMEM


def chunks_of(length):
    return (length + CHUNK - 1) // CHUNK


def spread_kernel(planes, mask_ref, len_ref, k_ref, v_ref, send_ref):
    nblocks = mask_ref.shape[0]
    holders = nblocks // planes
    me = lax.axis_index("seq")
    start = jnp.int32(0)
    for a in range(nblocks - 1):
        counted = (a < me) & (lax.rem(me, planes) == a % planes)
        start += jnp.where(counted, mask_ref[me, a] * chunks_of(len_ref[a]), 0)
    for chunk in range(PER_KEYS):
        holder = lax.rem(start + chunk, holders)
        row = (chunk // holders) * PAIR
        rows = slice(chunk * CHUNK, (chunk + 1) * CHUNK)
        send_ref[holder, row : row + CHUNK, :] = k_ref[rows, :]
        send_ref[holder, row + CHUNK : row + PAIR, :] = v_ref[rows, :]


def table_kernel(planes, mask_ref, len_ref, meta_ref, choice_ref):
    nblocks = mask_ref.shape[0]
    holders = nblocks // planes
    me = lax.axis_index("seq")
    counts = [chunks_of(len_ref[b]) for b in range(nblocks)]
    most = jnp.int32(0)
    mine = [jnp.int32(0) for _ in range(planes)]
    for b in range(nblocks):
        for plane in range(planes):
            total = jnp.int32(0)
            for a in range(plane, b, planes):
                total += mask_ref[b, a] * counts[a]
            most = jnp.maximum(most, total)
            mine[plane] = jnp.where(me == b, total, mine[plane])
            if plane == b % planes:
                meta_ref[b] = total
    for plane in range(planes):
        meta_ref[nblocks + plane] = mine[plane]
    slots = (most + holders - 1) // holders
    choice = jnp.int32(0)
    for size in SIZES[:-1]:
        choice += jnp.where(slots > size, 1, 0)
    choice_ref[0] = choice


def pack_kernel(planes, slots, mask_ref, len_ref, meta_ref, held_ref, send_ref, work):
    nblocks = mask_ref.shape[0]
    holders = nblocks // planes
    me = lax.axis_index("seq")
    mine, plane = me // planes, lax.rem(me, planes)
    work[...] = jnp.zeros_like(work)

    for y in range(holders):
        block = y * planes + plane
        start = meta_ref[block]
        count = chunks_of(len_ref[block])
        first = lax.rem(mine - start + BLOCK, holders)
        for k in range(PER_KEYS // holders):
            chunk = first + k * holders
            slot = jnp.minimum((start + chunk) // holders, slots - 1)
            row = pl.multiple_of(slot * CHUNK, CHUNK)
            used = jnp.where(chunk < count, 1, 0)
            key = held_ref[y, k * PAIR : k * PAIR + CHUNK, :]
            value = held_ref[y, k * PAIR + CHUNK : (k + 1) * PAIR, :]
            for j in range(y * planes + 1, nblocks):
                needed = mask_ref[j, block] * used
                if j < (y + 1) * planes:
                    needed = jnp.where(block < j, needed, 0)
                to = jnp.where(needed > 0, j, nblocks)
                work[to, pl.ds(row, CHUNK), :] = key
                work[to, pl.ds(slots * CHUNK + row, CHUNK), :] = value
    send_ref[...] = work[:nblocks]


def own_kernel(
    planes, slots, mask_ref, len_ref, meta_ref, q_ref, k_ref, v_ref, probe_ref,
    top_ref, total_ref, acc_ref, across_ref, down_ref, lastq_ref, probes_ref, own_s_ref, own_p_ref, vt,
):
    nblocks = mask_ref.shape[0]
    me = lax.axis_index("seq")
    length = len_ref[me]
    nheads = q_ref.shape[1] // DH
    scale = 1.0 / math.sqrt(DH)
    holders = nblocks // planes
    lane = lax.broadcasted_iota(jnp.int32, (1, slots * BLOCK), 1)
    source = ((lane.astype(jnp.float32) + 0.5) * (1.0 / (slots * CHUNK))).astype(jnp.int32)
    within = lane - source * (slots * CHUNK)
    row_at = (within // CHUNK * holders + source // planes) * CHUNK + within % CHUNK
    of_plane = source % planes
    row_id = lax.broadcasted_iota(jnp.int32, (CHUNK, DH), 0)
    allowed = jnp.zeros(lane.shape, jnp.int32)
    down_ref[...] = jnp.full(down_ref.shape, NEG, jnp.float32)
    for b in range(nblocks - 1):
        before = meta_ref[b]
        for plane in range(b % planes):
            before += meta_ref[nblocks + plane]
        used = jnp.where((mask_ref[me, b] > 0) & (b < me), len_ref[b], 0)
        row = row_at - meta_ref[b] * CHUNK
        allowed = jnp.where((of_plane == b % planes) & (row >= 0) & (row < used), 1, allowed)

        def one_chunk(c, carry):
            at = pl.multiple_of((before + c) * CHUNK, CHUNK)
            down_ref[pl.ds(at, CHUNK), :] = jnp.where(row_id < used - c * CHUNK, 0.0, NEG)
            return carry

        lax.fori_loop(0, chunks_of(used), one_chunk, 0)
    across_ref[...] = jnp.where(allowed > 0, 0.0, NEG)
    causal = lax.broadcasted_iota(jnp.int32, (BLOCK, BLOCK), 0) <= lax.broadcasted_iota(
        jnp.int32, (BLOCK, BLOCK), 1
    )
    vt[...] = jnp.transpose(v_ref[...].astype(jnp.float32)).astype(jnp.bfloat16)
    last = length - 1
    base = pl.multiple_of(last // CHUNK * CHUNK, CHUNK)
    picked = lax.broadcasted_iota(jnp.int32, (CHUNK, 1), 0) == last - base

    def one_head(h, carry):
        columns = pl.ds(pl.multiple_of(h * DH, DH), DH)
        scores = lax.dot_general(k_ref[...], q_ref[:, columns], NT, preferred_element_type=jnp.float32)
        scores = jnp.where(causal, scores, NEG)
        top = jnp.max(scores, axis=0, keepdims=True)
        w = jnp.exp((scores - top) * scale)
        top_ref[h] = top
        total_ref[h] = jnp.sum(w, axis=0, keepdims=True)
        acc_ref[h] = jnp.dot(vt[...], w.astype(jnp.bfloat16), preferred_element_type=jnp.float32)
        return carry

    lax.fori_loop(0, nheads, one_head, 0)
    for h in range(nheads):
        columns = slice(h * DH, (h + 1) * DH)
        near = q_ref[pl.ds(base, CHUNK), columns].astype(jnp.float32)
        lastq_ref[h : h + 1, :] = jnp.sum(jnp.where(picked, near, 0.0), axis=0, keepdims=True)
        probes_ref[h : h + 1, :] = probe_ref[:, columns].astype(jnp.float32)
    lastq = lastq_ref[...].astype(jnp.bfloat16)
    probes = probes_ref[...].astype(jnp.bfloat16)
    own_s = lax.dot_general(lastq, k_ref[...], NT, preferred_element_type=jnp.float32)
    inside = lax.broadcasted_iota(jnp.int32, (1, BLOCK), 1) < length
    own_s_ref[...] = jnp.where(inside, own_s, NEG)
    own_p_ref[...] = lax.dot_general(probes, v_ref[...], NT, preferred_element_type=jnp.float32)


def score_kernel(slots, got_ref, across_ref, lastq_ref, probes_ref, own_s_ref, own_p_ref, score_ref):
    nblocks = got_ref.shape[0]
    scale = 1.0 / math.sqrt(DH)
    half = slots * CHUNK
    lastq = lastq_ref[...].astype(jnp.bfloat16)
    probes = probes_ref[...].astype(jnp.bfloat16)
    keys = jnp.concatenate([got_ref[i, :half, :] for i in range(nblocks)], axis=0)
    vals = jnp.concatenate([got_ref[i, half:, :] for i in range(nblocks)], axis=0)
    scores = lax.dot_general(lastq, keys, NT, preferred_element_type=jnp.float32) + across_ref[...]
    products = lax.dot_general(probes, vals, NT, preferred_element_type=jnp.float32)
    own_s = own_s_ref[...]
    top = jnp.maximum(jnp.max(scores, axis=1, keepdims=True), jnp.max(own_s, axis=1, keepdims=True))
    w = jnp.exp((scores - top) * scale)
    own_w = jnp.exp((own_s - top) * scale)
    total = jnp.sum(w, axis=1, keepdims=True) + jnp.sum(own_w, axis=1, keepdims=True)
    mixed = jnp.sum(w * products, axis=1, keepdims=True) + jnp.sum(own_w * own_p_ref[...], axis=1, keepdims=True)
    score_ref[...] = jnp.full(score_ref.shape, jnp.sum(mixed / total), jnp.float32)


def attend_kernel(
    planes, slots, len_ref, meta_ref, q_ref, got_ref, down_ref, top_ref, total_ref, acc_ref, out_ref,
    keys, vals, kept, tops, totals, accs,
):
    length = len_ref[lax.axis_index("seq")]
    nblocks = len_ref.shape[0]
    nheads = q_ref.shape[1] // DH
    scale = 1.0 / math.sqrt(DH)
    holders = nblocks // planes
    half = slots * CHUNK
    count = jnp.int32(0)
    for plane in range(planes):
        for s in range(slots):
            for p in range(holders):
                at = pl.multiple_of((count + s * holders + p) * CHUNK, CHUNK)
                i = p * planes + plane
                keys[pl.ds(at, CHUNK), :] = got_ref[i, s * CHUNK : (s + 1) * CHUNK, :]
                vals[pl.ds(at, CHUNK), :] = got_ref[i, half + s * CHUNK : half + (s + 1) * CHUNK, :]
        if plane == planes - 1:
            tail = pl.multiple_of((count + slots * holders) * CHUNK, CHUNK)
            keys[pl.ds(tail, BLOCK), :] = jnp.zeros((BLOCK, DH), jnp.bfloat16)
            vals[pl.ds(tail, BLOCK), :] = jnp.zeros((BLOCK, DH), jnp.bfloat16)
        count += meta_ref[nblocks + plane]
    steps = (count + PER_KEYS - 1) // PER_KEYS
    for h in range(nheads):
        tops[h] = jnp.broadcast_to(top_ref[h], (8, BLOCK))

    def one_score(n, carry):
        at = pl.ds(pl.multiple_of(n * BLOCK, BLOCK), BLOCK)
        bias = down_ref[at, :]
        bias = jnp.concatenate([bias, bias], axis=1)
        for h in range(nheads):
            q = q_ref[:, h * DH : (h + 1) * DH]
            part = lax.dot_general(keys[at, :], q, NT, preferred_element_type=jnp.float32) + bias
            kept[n, h] = part
            tops[h] = jnp.maximum(tops[h], jnp.max(part.reshape(BLOCK // 8, 8, BLOCK), axis=0))
        return carry

    lax.fori_loop(0, steps, one_score, 0)
    for h in range(nheads):
        top = jnp.max(tops[h], axis=0, keepdims=True)
        tops[h] = jnp.broadcast_to(top, (8, BLOCK))
        factor = jnp.exp((top_ref[h] - top) * scale)
        row = lax.broadcasted_iota(jnp.int32, (8, BLOCK), 0)
        totals[h] = jnp.where(row == 0, total_ref[h] * factor, 0.0)
        accs[h] = acc_ref[h] * factor

    def one_mix(n, carry):
        at = pl.ds(pl.multiple_of(n * BLOCK, BLOCK), BLOCK)
        vt = jnp.transpose(vals[at, :].astype(jnp.float32)).astype(jnp.bfloat16)
        for h in range(nheads):
            w = jnp.exp((kept[n, h] - tops[h, :1, :]) * scale)
            totals[h] += jnp.sum(w.reshape(BLOCK // 8, 8, BLOCK), axis=0)
            accs[h] += jnp.dot(vt, w.astype(jnp.bfloat16), preferred_element_type=jnp.float32)
        return carry

    lax.fori_loop(0, steps, one_mix, 0)
    row_id = lax.broadcasted_iota(jnp.int32, (BLOCK, 1), 0)
    for h in range(nheads):
        total = jnp.sum(totals[h], axis=0, keepdims=True)
        result = jnp.transpose(accs[h] / total)
        out_ref[:, h * DH : (h + 1) * DH] = jnp.where(row_id < length, result, 0.0).astype(out_ref.dtype)


def on_device(planes, queries, keys, values, tree_mask, step_lengths, probe):
    nblocks = tree_mask.shape[0]
    holders = nblocks // planes
    nheads = queries.shape[1] // DH
    smem, vmem = pl.BlockSpec(memory_space=SMEM), pl.BlockSpec(memory_space=VMEM)
    f32, bf16 = jnp.float32, jnp.bfloat16
    shape = jax.ShapeDtypeStruct
    limit = lambda mib: pltpu.CompilerParams(vmem_limit_bytes=mib * 1024 * 1024)
    send = pl.pallas_call(
        functools.partial(spread_kernel, planes),
        out_shape=shape((holders, PER_KEYS // holders * PAIR, DH), bf16),
        in_specs=[smem, smem, vmem, vmem],
        out_specs=vmem,
        compiler_params=limit(8),
    )(tree_mask, step_lengths, keys, values)
    groups = [[y * planes + p for y in range(holders)] for p in range(planes)]
    held = lax.all_to_all(send, "seq", 0, 0, axis_index_groups=groups)
    meta, choice = pl.pallas_call(
        functools.partial(table_kernel, planes),
        out_shape=(shape((nblocks + planes,), jnp.int32), shape((1,), jnp.int32)),
        in_specs=[smem, smem],
        out_specs=(smem, smem),
        cost_estimate=pl.CostEstimate(flops=10**8, bytes_accessed=10**5, transcendentals=0),
        compiler_params=limit(8),
    )(tree_mask, step_lengths)

    def rest(slots, held, meta):
        packed = pl.pallas_call(
            functools.partial(pack_kernel, planes, slots),
            out_shape=shape((nblocks, slots * PAIR, DH), bf16),
            in_specs=[smem, smem, smem, vmem],
            out_specs=vmem,
            scratch_shapes=[VMEM((nblocks + 1, slots * PAIR, DH), bf16)],
            compiler_params=limit(16),
        )(tree_mask, step_lengths, meta, held)
        got = lax.all_to_all(packed, "seq", 0, 0)
        per_head = shape((nheads, 1, BLOCK), f32)
        small = shape((nheads, DH), f32)
        top, total, acc, across, down, lastq, probes, own_s, own_p = pl.pallas_call(
            functools.partial(own_kernel, planes, slots),
            out_shape=(
                per_head, per_head, shape((nheads, DH, BLOCK), f32), shape((1, slots * BLOCK), f32),
                shape((slots * BLOCK, DH), f32), small, small,
                shape((nheads, BLOCK), f32), shape((nheads, BLOCK), f32),
            ),
            in_specs=[smem, smem, smem, vmem, vmem, vmem, vmem],
            out_specs=(vmem,) * 9,
            scratch_shapes=[VMEM((DH, BLOCK), bf16)],
            cost_estimate=pl.CostEstimate(flops=10**9, bytes_accessed=5 * 10**6, transcendentals=10**6),
            compiler_params=limit(12),
        )(tree_mask, step_lengths, meta, queries, keys, values, probe.reshape(1, -1))
        score = pl.pallas_call(
            functools.partial(score_kernel, slots),
            out_shape=shape((lax.axis_size("mp"), 1, DH), f32),
            in_specs=[vmem] * 6,
            out_specs=vmem,
            compiler_params=limit(16),
        )(got, across, lastq, probes, own_s, own_p)
        parts = lax.all_to_all(score, "mp", 0, 0)
        attended = pl.pallas_call(
            functools.partial(attend_kernel, planes, slots),
            out_shape=shape(queries.shape, bf16),
            in_specs=[smem, smem] + [vmem] * 6,
            out_specs=vmem,
            scratch_shapes=[
                VMEM((slots * BLOCK + BLOCK, DH), bf16),
                VMEM((slots * BLOCK + BLOCK, DH), bf16),
                VMEM((slots, nheads, BLOCK, BLOCK), f32),
                VMEM((nheads, 8, BLOCK), f32),
                VMEM((nheads, 8, BLOCK), f32),
                VMEM((nheads, DH, BLOCK), f32),
            ],
            cost_estimate=pl.CostEstimate(flops=4 * 10**9, bytes_accessed=5 * 10**6, transcendentals=4 * 10**6),
            compiler_params=limit(10 + 2 * slots),
        )(step_lengths, meta, queries, got, down, top, total, acc)
        return attended, parts

    branches = [functools.partial(rest, s) for s in SIZES]
    attended, parts = lax.switch(choice[0], branches, held, meta)
    return attended, jnp.sum(parts[:, 0, :1], axis=0)


def solution(mesh):
    in_specs = (
        P(("leaf", "seq"), "mp"),
        P(("leaf", "seq"), "mp"),
        P(("leaf", "seq"), "mp"),
        P("leaf", None),
        P("leaf"),
        P("mp"),
    )
    out_specs = (P(("leaf", "seq"), "mp"), P(("leaf", "seq")))
    return jax.shard_map(
        functools.partial(on_device, 2), mesh=mesh, in_specs=in_specs, out_specs=out_specs, check_vma=False
    )
```

```python
import functools
import math

import jax
import jax.numpy as jnp
from jax import lax
from jax.experimental import pallas as pl
from jax.experimental.pallas import tpu as pltpu
from jax.sharding import PartitionSpec as P

DH = 128
BLOCK = 256
CHUNK = 16
PAIR = 2 * CHUNK
PER_KEYS = BLOCK // CHUNK
NEG = -1e30
NT = (((1,), (1,)), ((), ()))
SIZES = (3, 4, 5, 6, 7, 8, 11, 16)

VMEM = pltpu.VMEM
SMEM = pltpu.SMEM


def chunks_of(length):
    return (length + CHUNK - 1) // CHUNK


def entry(row_ref, index):
    row = row_ref[...].reshape(1, -1)
    at = lax.broadcasted_iota(jnp.int32, row.shape, 1) == index
    return jnp.sum(jnp.where(at, row, 0))


def spread_kernel(planes, mask_ref, len_ref, k_ref, v_ref, send_ref):
    nblocks = mask_ref.shape[0]
    holders = nblocks // planes
    me = lax.axis_index("seq")
    row = lax.broadcasted_iota(jnp.int32, mask_ref.shape, 0)
    column = lax.broadcasted_iota(jnp.int32, mask_ref.shape, 1)
    counted = (row == me) & (column < me) & (column % planes == lax.rem(me, planes))
    start = jnp.sum(jnp.where(counted, mask_ref[...] * chunks_of(len_ref[...].reshape(1, -1)), 0))
    for chunk in range(PER_KEYS):
        holder = lax.rem(start + chunk, holders)
        row = (chunk // holders) * PAIR
        rows = slice(chunk * CHUNK, (chunk + 1) * CHUNK)
        send_ref[holder, row : row + CHUNK, :] = k_ref[rows, :]
        send_ref[holder, row + CHUNK : row + PAIR, :] = v_ref[rows, :]


def table_kernel(planes, mask_ref, len_ref, meta_ref, choice_ref):
    nblocks = mask_ref.shape[0]
    holders = nblocks // planes
    me = lax.axis_index("seq")
    counts = [chunks_of(len_ref[b]) for b in range(nblocks)]
    most = jnp.int32(0)
    mine = [jnp.int32(0) for _ in range(planes)]
    for b in range(nblocks):
        for plane in range(planes):
            total = jnp.int32(0)
            for a in range(plane, b, planes):
                total += mask_ref[b, a] * counts[a]
            most = jnp.maximum(most, total)
            mine[plane] = jnp.where(me == b, total, mine[plane])
            if plane == b % planes:
                meta_ref[b] = total
    for plane in range(planes):
        meta_ref[nblocks + plane] = mine[plane]
    slots = (most + holders - 1) // holders
    choice = jnp.int32(0)
    for size in SIZES[:-1]:
        choice += jnp.where(slots > size, 1, 0)
    choice_ref[0] = choice


def pack_kernel(planes, slots, mask_ref, len_ref, meta_ref, held_ref, send_ref, work):
    nblocks = mask_ref.shape[0]
    holders = nblocks // planes
    me = lax.axis_index("seq")
    mine, plane = me // planes, lax.rem(me, planes)
    work[...] = jnp.zeros_like(work)

    for y in range(holders):
        block = y * planes + plane
        start = meta_ref[block]
        count = chunks_of(len_ref[block])
        first = lax.rem(mine - start + BLOCK, holders)
        for k in range(PER_KEYS // holders):
            chunk = first + k * holders
            slot = jnp.minimum((start + chunk) // holders, slots - 1)
            row = pl.multiple_of(slot * CHUNK, CHUNK)
            used = jnp.where(chunk < count, 1, 0)
            key = held_ref[y, k * PAIR : k * PAIR + CHUNK, :]
            value = held_ref[y, k * PAIR + CHUNK : (k + 1) * PAIR, :]
            for j in range(y * planes + 1, nblocks):
                needed = mask_ref[j, block] * used
                if j < (y + 1) * planes:
                    needed = jnp.where(block < j, needed, 0)
                to = jnp.where(needed > 0, j, nblocks)
                work[to, pl.ds(row, CHUNK), :] = key
                work[to, pl.ds(slots * CHUNK + row, CHUNK), :] = value
    send_ref[...] = work[:nblocks]


def own_kernel(
    planes, slots, mask_ref, len_ref, meta_ref, q_ref, k_ref, v_ref, probe_ref,
    top_ref, total_ref, acc_ref, across_ref, down_ref, lastq_ref, probes_ref, own_s_ref, own_p_ref, vt,
):
    nblocks = mask_ref.shape[0]
    me = lax.axis_index("seq")
    length = len_ref[me]
    nheads = q_ref.shape[1] // DH
    scale = 1.0 / math.sqrt(DH)
    holders = nblocks // planes
    lane = lax.broadcasted_iota(jnp.int32, (1, slots * BLOCK), 1)
    source = ((lane.astype(jnp.float32) + 0.5) * (1.0 / (slots * CHUNK))).astype(jnp.int32)
    within = lane - source * (slots * CHUNK)
    row_at = (within // CHUNK * holders + source // planes) * CHUNK + within % CHUNK
    of_plane = source % planes
    row_id = lax.broadcasted_iota(jnp.int32, (CHUNK, DH), 0)
    allowed = jnp.zeros(lane.shape, jnp.int32)
    down_ref[...] = jnp.full(down_ref.shape, NEG, jnp.float32)
    for b in range(nblocks - 1):
        before = meta_ref[b]
        for plane in range(b % planes):
            before += meta_ref[nblocks + plane]
        used = jnp.where((mask_ref[me, b] > 0) & (b < me), len_ref[b], 0)
        row = row_at - meta_ref[b] * CHUNK
        allowed = jnp.where((of_plane == b % planes) & (row >= 0) & (row < used), 1, allowed)

        def one_chunk(c, carry):
            at = pl.multiple_of((before + c) * CHUNK, CHUNK)
            down_ref[pl.ds(at, CHUNK), :] = jnp.where(row_id < used - c * CHUNK, 0.0, NEG)
            return carry

        lax.fori_loop(0, chunks_of(used), one_chunk, 0)
    across_ref[...] = jnp.where(allowed > 0, 0.0, NEG)
    causal = lax.broadcasted_iota(jnp.int32, (BLOCK, BLOCK), 0) <= lax.broadcasted_iota(
        jnp.int32, (BLOCK, BLOCK), 1
    )
    vt[...] = jnp.transpose(v_ref[...].astype(jnp.float32)).astype(jnp.bfloat16)
    last = length - 1
    base = pl.multiple_of(last // CHUNK * CHUNK, CHUNK)
    picked = lax.broadcasted_iota(jnp.int32, (CHUNK, 1), 0) == last - base

    def one_head(h, carry):
        columns = pl.ds(pl.multiple_of(h * DH, DH), DH)
        scores = lax.dot_general(k_ref[...], q_ref[:, columns], NT, preferred_element_type=jnp.float32)
        scores = jnp.where(causal, scores, NEG)
        top = jnp.max(scores, axis=0, keepdims=True)
        w = jnp.exp((scores - top) * scale)
        top_ref[h] = top
        total_ref[h] = jnp.sum(w, axis=0, keepdims=True)
        acc_ref[h] = jnp.dot(vt[...], w.astype(jnp.bfloat16), preferred_element_type=jnp.float32)
        return carry

    lax.fori_loop(0, nheads, one_head, 0)
    for h in range(nheads):
        columns = slice(h * DH, (h + 1) * DH)
        near = q_ref[pl.ds(base, CHUNK), columns].astype(jnp.float32)
        lastq_ref[h : h + 1, :] = jnp.sum(jnp.where(picked, near, 0.0), axis=0, keepdims=True)
        probes_ref[h : h + 1, :] = probe_ref[:, columns].astype(jnp.float32)
    lastq = lastq_ref[...].astype(jnp.bfloat16)
    probes = probes_ref[...].astype(jnp.bfloat16)
    own_s = lax.dot_general(lastq, k_ref[...], NT, preferred_element_type=jnp.float32)
    inside = lax.broadcasted_iota(jnp.int32, (1, BLOCK), 1) < length
    own_s_ref[...] = jnp.where(inside, own_s, NEG)
    own_p_ref[...] = lax.dot_general(probes, v_ref[...], NT, preferred_element_type=jnp.float32)


def score_kernel(slots, got_ref, across_ref, lastq_ref, probes_ref, own_s_ref, own_p_ref, score_ref):
    nblocks = got_ref.shape[0]
    scale = 1.0 / math.sqrt(DH)
    half = slots * CHUNK
    lastq = lastq_ref[...].astype(jnp.bfloat16)
    probes = probes_ref[...].astype(jnp.bfloat16)
    keys = jnp.concatenate([got_ref[i, :half, :] for i in range(nblocks)], axis=0)
    vals = jnp.concatenate([got_ref[i, half:, :] for i in range(nblocks)], axis=0)
    scores = lax.dot_general(lastq, keys, NT, preferred_element_type=jnp.float32) + across_ref[...]
    products = lax.dot_general(probes, vals, NT, preferred_element_type=jnp.float32)
    own_s = own_s_ref[...]
    top = jnp.maximum(jnp.max(scores, axis=1, keepdims=True), jnp.max(own_s, axis=1, keepdims=True))
    w = jnp.exp((scores - top) * scale)
    own_w = jnp.exp((own_s - top) * scale)
    total = jnp.sum(w, axis=1, keepdims=True) + jnp.sum(own_w, axis=1, keepdims=True)
    mixed = jnp.sum(w * products, axis=1, keepdims=True) + jnp.sum(own_w * own_p_ref[...], axis=1, keepdims=True)
    score_ref[...] = jnp.full(score_ref.shape, jnp.sum(mixed / total), jnp.float32)


def attend_kernel(
    planes, slots, len_ref, meta_ref, q_ref, got_ref, down_ref, top_ref, total_ref, acc_ref, out_ref,
    keys, vals, kept, tops, totals, accs,
):
    length = entry(len_ref, lax.axis_index("seq"))
    nblocks = len_ref.shape[0]
    nheads = q_ref.shape[1] // DH
    scale = 1.0 / math.sqrt(DH)
    holders = nblocks // planes
    half = slots * CHUNK
    count = jnp.int32(0)
    for plane in range(planes):
        for s in range(slots):
            for p in range(holders):
                at = pl.multiple_of((count + s * holders + p) * CHUNK, CHUNK)
                i = p * planes + plane
                keys[pl.ds(at, CHUNK), :] = got_ref[i, s * CHUNK : (s + 1) * CHUNK, :]
                vals[pl.ds(at, CHUNK), :] = got_ref[i, half + s * CHUNK : half + (s + 1) * CHUNK, :]
        if plane == planes - 1:
            tail = pl.multiple_of((count + slots * holders) * CHUNK, CHUNK)
            keys[pl.ds(tail, BLOCK), :] = jnp.zeros((BLOCK, DH), jnp.bfloat16)
            vals[pl.ds(tail, BLOCK), :] = jnp.zeros((BLOCK, DH), jnp.bfloat16)
        count += entry(meta_ref, nblocks + plane)
    steps = (count + PER_KEYS - 1) // PER_KEYS
    for h in range(nheads):
        tops[h] = jnp.broadcast_to(top_ref[h], (8, BLOCK))

    def one_score(n, carry):
        at = pl.ds(pl.multiple_of(n * BLOCK, BLOCK), BLOCK)
        bias = down_ref[at, :]
        bias = jnp.concatenate([bias, bias], axis=1)
        for h in range(nheads):
            q = q_ref[:, h * DH : (h + 1) * DH]
            part = lax.dot_general(keys[at, :], q, NT, preferred_element_type=jnp.float32) + bias
            kept[n, h] = part
            tops[h] = jnp.maximum(tops[h], jnp.max(part.reshape(BLOCK // 8, 8, BLOCK), axis=0))
        return carry

    lax.fori_loop(0, steps, one_score, 0)
    for h in range(nheads):
        top = jnp.max(tops[h], axis=0, keepdims=True)
        tops[h] = jnp.broadcast_to(top, (8, BLOCK))
        factor = jnp.exp((top_ref[h] - top) * scale)
        row = lax.broadcasted_iota(jnp.int32, (8, BLOCK), 0)
        totals[h] = jnp.where(row == 0, total_ref[h] * factor, 0.0)
        accs[h] = acc_ref[h] * factor

    def one_mix(n, carry):
        at = pl.ds(pl.multiple_of(n * BLOCK, BLOCK), BLOCK)
        vt = jnp.transpose(vals[at, :].astype(jnp.float32)).astype(jnp.bfloat16)
        for h in range(nheads):
            w = jnp.exp((kept[n, h] - tops[h, :1, :]) * scale)
            totals[h] += jnp.sum(w.reshape(BLOCK // 8, 8, BLOCK), axis=0)
            accs[h] += jnp.dot(vt, w.astype(jnp.bfloat16), preferred_element_type=jnp.float32)
        return carry

    lax.fori_loop(0, steps, one_mix, 0)
    row_id = lax.broadcasted_iota(jnp.int32, (BLOCK, 1), 0)
    for h in range(nheads):
        total = jnp.sum(totals[h], axis=0, keepdims=True)
        result = jnp.transpose(accs[h] / total)
        out_ref[:, h * DH : (h + 1) * DH] = jnp.where(row_id < length, result, 0.0).astype(out_ref.dtype)


def on_device(planes, queries, keys, values, tree_mask, step_lengths, probe):
    nblocks = tree_mask.shape[0]
    holders = nblocks // planes
    nheads = queries.shape[1] // DH
    smem, vmem = pl.BlockSpec(memory_space=SMEM), pl.BlockSpec(memory_space=VMEM)
    f32, bf16 = jnp.float32, jnp.bfloat16
    shape = jax.ShapeDtypeStruct
    limit = lambda mib: pltpu.CompilerParams(vmem_limit_bytes=mib * 1024 * 1024)
    send = pl.pallas_call(
        functools.partial(spread_kernel, planes),
        out_shape=shape((holders, PER_KEYS // holders * PAIR, DH), bf16),
        in_specs=[vmem] * 4,
        out_specs=vmem,
        compiler_params=limit(8),
    )(tree_mask, step_lengths, keys, values)
    groups = [[y * planes + p for y in range(holders)] for p in range(planes)]
    held = lax.all_to_all(send, "seq", 0, 0, axis_index_groups=groups)
    meta, choice = pl.pallas_call(
        functools.partial(table_kernel, planes),
        out_shape=(shape((nblocks + planes,), jnp.int32), shape((1,), jnp.int32)),
        in_specs=[smem, smem],
        out_specs=(smem, smem),
        cost_estimate=pl.CostEstimate(flops=10**8, bytes_accessed=10**5, transcendentals=0),
        compiler_params=limit(8),
    )(tree_mask, step_lengths)

    def rest(slots, held, meta):
        packed = pl.pallas_call(
            functools.partial(pack_kernel, planes, slots),
            out_shape=shape((nblocks, slots * PAIR, DH), bf16),
            in_specs=[smem, smem, smem, vmem],
            out_specs=vmem,
            scratch_shapes=[VMEM((nblocks + 1, slots * PAIR, DH), bf16)],
            compiler_params=limit(16),
        )(tree_mask, step_lengths, meta, held)
        got = lax.all_to_all(packed, "seq", 0, 0)
        per_head = shape((nheads, 1, BLOCK), f32)
        small = shape((nheads, DH), f32)
        top, total, acc, across, down, lastq, probes, own_s, own_p = pl.pallas_call(
            functools.partial(own_kernel, planes, slots),
            out_shape=(
                per_head, per_head, shape((nheads, DH, BLOCK), f32), shape((1, slots * BLOCK), f32),
                shape((slots * BLOCK, DH), f32), small, small,
                shape((nheads, BLOCK), f32), shape((nheads, BLOCK), f32),
            ),
            in_specs=[smem, smem, smem, vmem, vmem, vmem, vmem],
            out_specs=(vmem,) * 9,
            scratch_shapes=[VMEM((DH, BLOCK), bf16)],
            cost_estimate=pl.CostEstimate(flops=10**9, bytes_accessed=5 * 10**6, transcendentals=10**6),
            compiler_params=limit(12),
        )(tree_mask, step_lengths, meta, queries, keys, values, probe.reshape(1, -1))
        score = pl.pallas_call(
            functools.partial(score_kernel, slots),
            out_shape=shape((lax.axis_size("mp"), 1, DH), f32),
            in_specs=[vmem] * 6,
            out_specs=vmem,
            compiler_params=limit(16),
        )(got, across, lastq, probes, own_s, own_p)
        parts = lax.all_to_all(score, "mp", 0, 0)
        attended = pl.pallas_call(
            functools.partial(attend_kernel, planes, slots),
            out_shape=shape(queries.shape, bf16),
            in_specs=[vmem] * 8,
            out_specs=vmem,
            scratch_shapes=[
                VMEM((slots * BLOCK + BLOCK, DH), bf16),
                VMEM((slots * BLOCK + BLOCK, DH), bf16),
                VMEM((slots, nheads, BLOCK, BLOCK), f32),
                VMEM((nheads, 8, BLOCK), f32),
                VMEM((nheads, 8, BLOCK), f32),
                VMEM((nheads, DH, BLOCK), f32),
            ],
            cost_estimate=pl.CostEstimate(flops=4 * 10**9, bytes_accessed=5 * 10**6, transcendentals=4 * 10**6),
            compiler_params=limit(10 + 2 * slots),
        )(step_lengths, meta, queries, got, down, top, total, acc)
        return attended, parts

    branches = [functools.partial(rest, s) for s in SIZES]
    attended, parts = lax.switch(choice[0], branches, held, meta)
    return attended, jnp.sum(parts[:, 0, :1], axis=0)


def solution(mesh):
    in_specs = (
        P(("leaf", "seq"), "mp"),
        P(("leaf", "seq"), "mp"),
        P(("leaf", "seq"), "mp"),
        P("leaf", None),
        P("leaf"),
        P("mp"),
    )
    out_specs = (P(("leaf", "seq"), "mp"), P(("leaf", "seq")))
    return jax.shard_map(
        functools.partial(on_device, 2), mesh=mesh, in_specs=in_specs, out_specs=out_specs, check_vma=False
    )
```
